32 devices in a mesh: passage: 8 (over z, y), span: 4 (over x, core).
Axes of the slice: x: 2, y: 2, z: 4, core: 2. Of those that a mesh axis runs over, the one named last changes fastest.
Arguments:
- grad_rows: float32 [16384, 3, 128], P(('passage', 'span')), may hold values from -6 to 6
- dest_rank: int32 [16384, 1], P(('passage', 'span')), may hold values from 0 to 3; in each aligned block of 512 rows (0 to 511, 512 to 1023, ...) at most 256 rows name the same one
- dest_block: int32 [16384], P(('passage', 'span')), may hold values from 0 to 255
- cell_class: int32 [64, 64, 256], P('passage', 'span'), may hold values from 0 to 15
- class_stiffness: float32 [16], replicated, may hold values from 0.05 to 1
Outputs:
- update: float32 [3, 64, 64, 256], P(None, 'passage', 'span')
The draws below stay inside these ranges and needn't reach their ends.
Inputs may be any that keep to these rules, and one draw needn't show every extreme that they name: `dest_rank`: the rows of one device name each radial index at most 256 times, and exactly 256 times for some index of some devices.
All inputs are finite; a program needn't handle non-finite values.
Results may differ from the reference program's by a relative error of at most 0.00007.
Values sent between devices are 32-bit elements; how exact they have to be, the bound alone decides.
A program may use at most 64 MiB of HBM per device.

```python
import math
import jax
import jax.numpy as jnp
import numpy as np
from jax import lax

CX = 8
CY = 16
CZ = 256
ROWS_DEV = 512
NCLASS = 16
NPRE = 2
NPOST = 2
NCOARSE = 4
CAP = 256
NX = 64
NY = 64
NZ = 256
BLOCKS = 256
ROWS = 16384
N_PASSAGE = 8
N_SPAN = 4


def touch_ends(values, key, smallest, top_value):
    spot = [jax.random.randint(jax.random.fold_in(key, axis), (), 0, length) for axis, length in enumerate(values.shape)]
    longest = values.shape.index(max(values.shape))
    beside = spot[:longest] + [(spot[longest] + 1) % values.shape[longest]] + spot[longest + 1:]
    return values.at[tuple(spot)].set(smallest).at[tuple(beside)].set(top_value)


def levels(rng, extent, pieces, low, largest):
    factor_of = 1.0
    for position, blocks in pieces:
        draws = jax.random.uniform(jax.random.fold_in(jax.random.fold_in(rng, 6), position), (blocks,), jnp.float32, low / len(pieces), largest / len(pieces))
        factor_of = factor_of * jnp.repeat(jnp.exp(draws), extent[position] // blocks).reshape((-1,) + (1,) * (len(extent) - 1 - position))
    return factor_of


def assign_block(stream_key, own, number, rows, number_of, top, bound, lean):
    ranking = jax.random.permutation(stream_key, number_of)
    crowded, common = load_shares(number_of, rows * top, bound, lean, True), load_shares(number_of, rows * top, bound, lean, False)
    places = jnp.arange(number_of)

    def named(lengths, offset_by):
        used = int((lengths > 0).sum())
        fixed = max(1, used // 4)
        moved = fixed + (places - fixed + offset_by * (used - fixed)) % max(1, number_of - fixed)
        return jnp.zeros((number_of,), jnp.int32).at[ranking[jnp.where(places < fixed, places, moved)]].set(jnp.asarray(lengths, jnp.int32))

    lengths = jnp.where(number % 4 == 0, named(crowded, number // 4), named(common, number - number // 4 - 1))
    mixed = jax.random.permutation(jax.random.fold_in(own, 3), number_of)
    source_of, taker = mixed[0:number_of // 2 * 2:2], mixed[1:number_of // 2 * 2:2]
    slack = jnp.minimum(lengths[source_of] - 1, bound - lengths[taker]) // 2
    slack = jnp.where((source_of == ranking[0]) | (taker == ranking[0]) | (lengths[taker] == 0), 0, jnp.maximum(slack, 0))
    moved = jax.random.randint(jax.random.fold_in(own, 4), (number_of // 2,), 0, 1 << 20) % (slack + 1)
    lengths = lengths.at[source_of].add(-moved).at[taker].add(moved)
    items = jnp.searchsorted(jnp.cumsum(lengths), jnp.arange(rows * top), side="right").astype(jnp.int32)
    table = items.reshape(top, rows).T
    table = table[jax.random.permutation(jax.random.fold_in(own, 1), rows)]
    offset_by = jax.random.randint(jax.random.fold_in(own, 2), (rows, 1), 0, top)
    return jnp.take_along_axis(table, (jnp.arange(top)[None, :] + offset_by) % top, axis=1)


def load_shares(count, total, bound, slope, full):
    loads = [(1 << 20) // math.isqrt(rank ** slope) + 1 for rank in range(1, count + 1)]
    largest = bound if full else min(bound, max(-(-total // count), total * loads[0] // sum(loads)))
    least = 1 if total - largest >= count - 1 else 0
    given, spare = [largest] + [least] * (count - 1), total - largest - least * (count - 1)
    while spare > 0:
        movable = [i for i in range(1, count) if given[i] < largest] or [i for i in range(1, count) if given[i] < bound]
        pool, remaining = sum([loads[i] for i in movable]), spare
        for i in movable:
            extra = min(bound - given[i], max(1, remaining * loads[i] // pool), spare)
            given[i] = given[i] + extra
            spare = spare - extra
    return np.array(given)


def noise(key, extent, scale, reach, cuts=(), kind=jnp.bfloat16):
    drawn = jax.random.normal(key, extent, jnp.float32) * scale
    if len(cuts) > 0:
        drawn = levels(key, extent, cuts, -0.22, 0.18) * drawn
    return jnp.clip(drawn, min=-reach, max=reach).astype(kind)


def setup_inputs(seed: int = 0) -> dict:
    streams_of = jax.random.split(jax.random.key(seed), 6)
    grad_rows = noise(streams_of[0], (ROWS, 3, 128), 1.0, 6.0, ((0, 32),), jnp.float32)
    dest_rank_keys = jax.random.split(jax.random.fold_in(streams_of[1], 1), ROWS // ROWS_DEV)
    dest_rank_turns = jax.random.permutation(jax.random.fold_in(streams_of[1], 3), ROWS // ROWS_DEV)
    dest_rank = jax.vmap(lambda own, number: assign_block(jax.random.fold_in(streams_of[1], 2), own, number, ROWS_DEV, N_SPAN, 1, CAP, 2))(dest_rank_keys, dest_rank_turns).reshape((ROWS, 1))
    dest_block = touch_ends(jax.random.randint(streams_of[2], (ROWS,), 0, BLOCKS), jax.random.fold_in(streams_of[2], 1), 0, BLOCKS - 1).astype(jnp.int32)
    cell_class = touch_ends(jax.random.randint(streams_of[3], (NX, NY, NZ), 0, NCLASS), jax.random.fold_in(streams_of[3], 1), 0, NCLASS - 1).astype(jnp.int32)
    class_stiffness = jnp.clip(jnp.exp(jax.random.uniform(streams_of[4], (NCLASS,), jnp.float32, math.log(0.05), math.log(1.0))), 0.05, 1.0)
    return dict(grad_rows=grad_rows, dest_rank=dest_rank, dest_block=dest_block, cell_class=cell_class, class_stiffness=class_stiffness)


damping = 0.8
mass_share = 0.02


def pair_sums(values, along):
    new_shape = list(values.shape)
    new_shape[along:along + 1] = [new_shape[along] // 2, 2]
    return values.reshape(new_shape).sum(along + 1)


def every_other(values, along, offset):
    return lax.slice_in_dim(values, offset, values.shape[along], 2, along)


def face_weights(padded):
    stiffness = padded[1:-1, 1:-1]
    along_z = jnp.pad(stiffness, ((0, 0), (0, 0), (1, 1)), mode="edge")
    return (stiffness + padded[:-2, 1:-1], stiffness + padded[2:, 1:-1],
            stiffness + padded[1:-1, :-2], stiffness + padded[1:-1, 2:],
            stiffness + along_z[..., :-2], stiffness + along_z[..., 2:],
            mass_share * stiffness)


def coarsen(weights):
    lower_x, upper_x, lower_y, upper_y, lower_z, upper_z, masses = weights
    return (pair_sums(pair_sums(every_other(lower_x, 0, 0), 1), 2),
            pair_sums(pair_sums(every_other(upper_x, 0, 1), 1), 2),
            pair_sums(pair_sums(every_other(lower_y, 1, 0), 0), 2),
            pair_sums(pair_sums(every_other(upper_y, 1, 1), 0), 2),
            pair_sums(pair_sums(every_other(lower_z, 2, 0), 0), 1),
            pair_sums(pair_sums(every_other(upper_z, 2, 1), 0), 1),
            pair_sums(pair_sums(pair_sums(masses, 0), 1), 2))


def diagonal_of(weights):
    running = weights[0]
    for member in weights[1:]:
        running = running + member
    return running


def neighbours(field, padded, weights):
    lower_x, upper_x, lower_y, upper_y, lower_z, upper_z, masses = weights
    shifted = jnp.pad(field, ((0, 0), (0, 0), (0, 0), (1, 1)))
    return (lower_x * padded[:, :-2, 1:-1] + upper_x * padded[:, 2:, 1:-1]
            + lower_y * padded[:, 1:-1, :-2] + upper_y * padded[:, 1:-1, 2:]
            + lower_z * shifted[..., :-2] + upper_z * shifted[..., 2:])


def relax_once(field, source, padded, weights, diagonal):
    residue = source - (diagonal * field - neighbours(field, padded, weights))
    return field + damping * residue / diagonal


def prolong(values):
    return jnp.repeat(jnp.repeat(jnp.repeat(values, 2, 1), 2, 2), 2, 3)


def loop_pad(field):
    wrapped = jnp.concatenate([field[:, -1:], field, field[:, :1]], 1)
    return jnp.pad(wrapped, ((0, 0), (0, 0), (1, 1), (0, 0)))


def reference(grad_rows, dest_rank, dest_block, cell_class, class_stiffness):
    owner_part = jnp.arange(ROWS, dtype=jnp.int32) // (ROWS_DEV * N_SPAN)
    target = (owner_part * N_SPAN + dest_rank[:, 0]) * BLOCKS + dest_block
    summed = jax.ops.segment_sum(grad_rows.reshape(ROWS, 3 * 128), target,
                                 num_segments=N_PASSAGE * N_SPAN * BLOCKS)
    summed = summed.reshape(N_PASSAGE, N_SPAN, BLOCKS, 3, 128).transpose(3, 0, 1, 2, 4)
    summed = summed.reshape(3, N_PASSAGE, N_SPAN, CX, CY, CZ)
    source = summed.transpose(0, 1, 3, 2, 4, 5).reshape(3, NX, NY, NZ)
    stiffness = class_stiffness[cell_class]
    wrapped = jnp.concatenate([stiffness[-1:], stiffness, stiffness[:1]], 0)
    stiff_pad = jnp.pad(wrapped, ((0, 0), (1, 1), (0, 0)), mode="edge")
    weights = face_weights(stiff_pad)
    diagonal = diagonal_of(weights)
    field = damping * source / diagonal
    for sweep_count in range(NPRE - 1):
        field = relax_once(field, source, loop_pad(field), weights, diagonal)
    residue = source - (diagonal * field - neighbours(field, loop_pad(field), weights))
    coarse_source = pair_sums(pair_sums(pair_sums(residue, 1), 2), 3)
    coarse_weights = coarsen(weights)
    coarse_diagonal = diagonal_of(coarse_weights)
    correction = damping * coarse_source / coarse_diagonal
    for sweep_count in range(NCOARSE - 1):
        correction = relax_once(correction, coarse_source, loop_pad(correction), coarse_weights, coarse_diagonal)
    field = field + prolong(correction)
    for sweep_count in range(NPOST):
        field = relax_once(field, source, loop_pad(field), weights, diagonal)
    return field
```

```python
import functools

import jax
import jax.numpy as jnp
from jax import lax
from jax.experimental import pallas as pl
from jax.experimental.pallas import tpu as pltpu
from jax.sharding import PartitionSpec as P

damping = 0.8
mass_share = 0.02
HALO_S = 7
HALO_F = 3
HALO_C = 4
DIRS = [(dx, dy) for dx in (-1, 0, 1) for dy in (-1, 0, 1) if (dx, dy) != (0, 0)]
MESH = pl.DeviceIdType.MESH


def split2(values):
    high = values.astype(jnp.bfloat16)
    low = (values - high.astype(jnp.float32)).astype(jnp.bfloat16)
    return high, low


def dot(a, b):
    return jnp.dot(a, b, preferred_element_type=jnp.float32)


def as_bf16(mask):
    return jnp.where(mask, 1.0, 0.0).astype(jnp.bfloat16)


def kernel(
    passages, spans, key_ref, rows_ref, class_ref, table_ref, out_ref,
    split_ref, psend, srecv, rsend, rrecv, acc, stiff, fine, fine1, coarse,
    a_ref, d_ref, ca_ref, cd_ref, tmp, tmp2, own_s,
    sib_send, sib_recv, rem_send, rem_recv,
    st_send, st_recv, f_send, f_recv, c_send, c_recv,
):
    nx, ny, nz = class_ref.shape
    half = nz // 2
    blocks = nx * ny * 2
    nrows = rows_ref.shape[1]
    pairs = spans // 2
    p = lax.axis_index("passage")
    s = lax.axis_index("span")
    pair = s // 2
    core = s % 2
    sib = pair * 2 + 1 - core
    at_lower = s == 0
    at_upper = s == spans - 1

    def side(dx):
        return lax.rem(p + dx + passages, passages)

    def inside(dy):
        if dy == 0:
            return None
        return s + dy < spans if dy > 0 else s + dy >= 0

    def guarded(cond, action):
        if cond is None:
            action()
        else:
            pl.when(cond)(action)

    barrier = pltpu.get_barrier_semaphore()
    for dx, dy in DIRS:
        def greet(dx=dx, dy=dy):
            pl.semaphore_signal(barrier, inc=1, device_id=(side(dx), s + dy), device_id_type=MESH)
        guarded(inside(dy), greet)
    pl.semaphore_signal(barrier, inc=1, device_id=(p, sib), device_id_type=MESH)
    for q in range(1, pairs):
        pl.semaphore_signal(
            barrier, inc=1, device_id=(p, lax.rem(pair + q, pairs) * 2 + core), device_id_type=MESH
        )

    def halo(buffer, halo_x, own_x, own_y, send, recv):
        def spans_of(d, width, own, step):
            if d == 0:
                return (width, width, own)
            if d > 0:
                return (own + width - step, 0 + width - step, step)
            return (width, width + own, step)

        copies = []
        for k, (dx, dy) in enumerate(DIRS):
            sx, tx, lx = spans_of(dx, halo_x, own_x, halo_x)
            sy, ty, ly = spans_of(dy, 8, own_y, 8)
            copies.append(
                (dy, pltpu.make_async_remote_copy(
                    src_ref=buffer.at[pl.ds(sx, lx), pl.ds(sy, ly), :],
                    dst_ref=buffer.at[pl.ds(tx, lx), pl.ds(ty, ly), :],
                    send_sem=send.at[k],
                    recv_sem=recv.at[k],
                    device_id=(side(dx), s + dy),
                    device_id_type=MESH,
                ))
            )
        return copies

    def start(copies):
        for dy, copy in copies:
            guarded(inside(dy), copy.start)

    def finish(copies):
        for dy, copy in copies:
            guarded(inside(-dy), copy.wait_recv)
            guarded(inside(dy), copy.wait_send)

    wide_r = lax.broadcasted_iota(jnp.int32, (nz, nz), 0)
    wide_c = lax.broadcasted_iota(jnp.int32, (nz, nz), 1)
    to_halves = as_bf16(wide_r == jnp.where(wide_c < half, 2 * wide_c, 2 * wide_c - (nz - 1)))
    classes = class_ref[...].reshape(nx * ny, nz).astype(jnp.float32).astype(jnp.bfloat16)
    classes = dot(classes, to_halves)
    values = jnp.zeros_like(classes)
    for k in range(table_ref.shape[1]):
        values = jnp.where(classes == float(k), table_ref[0, k], values)
    stiff[pl.ds(HALO_S, nx), pl.ds(8, ny), :] = values.reshape(nx, ny, nz)

    in_r, in_c = wide_r % half, wide_c % half
    rows_perm = as_bf16(
        (wide_r // half == wide_c // half)
        & (in_r == jnp.where(in_c < half // 2, 2 * in_c, 2 * in_c - (half - 1)))
    )
    for c in range(3):
        high, low = split2(rows_ref[c])
        parts = jnp.concatenate([high, low], axis=1)
        split_ref[c] = dot(parts, rows_perm).astype(jnp.bfloat16)

    block_iota = lax.broadcasted_iota(jnp.int32, (blocks, nrows), 0)
    key = key_ref[...]

    def chosen(target):
        return as_bf16(block_iota + target * blocks == key)

    def partial(hot, c):
        both = dot(hot, split_ref[c])
        return both[:, :half] + both[:, half:]

    n_greet = 3 * 2 + 2 + 1 + (pairs - 1)
    missing = 3 * (jnp.where(at_lower, 1, 0) + jnp.where(at_upper, 1, 0))
    pl.semaphore_wait(barrier, n_greet - missing)

    stiff_copies = halo(stiff, HALO_S, nx, ny, st_send, st_recv)
    start(stiff_copies)

    def to_sib(q, c):
        return pltpu.make_async_remote_copy(
            src_ref=psend.at[q, c], dst_ref=srecv.at[q, c],
            send_sem=sib_send.at[q, c], recv_sem=sib_recv.at[q, c],
            device_id=(p, sib), device_id_type=MESH,
        )

    def to_rem(q, c):
        return pltpu.make_async_remote_copy(
            src_ref=rsend.at[q - 1, c], dst_ref=rrecv.at[q - 1, c],
            send_sem=rem_send.at[q - 1, c], recv_sem=rem_recv.at[q - 1, c],
            device_id=(p, lax.rem(pair + q, pairs) * 2 + core), device_id_type=MESH,
        )

    for q in list(range(1, pairs)):
        target = lax.rem(pair + q, pairs) * 2
        hot = chosen(target + 1 - core)
        for c in range(3):
            psend[q, c] = partial(hot, c)
            to_sib(q, c).start()
    for q in range(1, pairs):
        target = lax.rem(pair + q, pairs) * 2
        hot = chosen(target + core)
        for c in range(3):
            own = partial(hot, c)
            to_sib(q, c).wait_recv()
            rsend[q - 1, c] = own + srecv[q, c]
            to_rem(q, c).start()
    hot = chosen(pair * 2 + 1 - core)
    for c in range(3):
        psend[0, c] = partial(hot, c)
        to_sib(0, c).start()
    hot = chosen(s)
    for c in range(3):
        acc[c] = partial(hot, c)

    finish(stiff_copies)
    total_x = nx + 2 * HALO_S

    @pl.when(at_lower)
    def _():
        def body(i, carry):
            stiff[i, pl.ds(0, 8), :] = jnp.broadcast_to(stiff[i, pl.ds(8, 1), :], (8, nz))
            return carry
        lax.fori_loop(0, total_x, body, 0)

    @pl.when(at_upper)
    def _():
        def body(i, carry):
            stiff[i, pl.ds(8 + ny, 8), :] = jnp.broadcast_to(
                stiff[i, pl.ds(7 + ny, 1), :], (8, nz)
            )
            return carry
        lax.fori_loop(0, total_x, body, 0)

    ey = ny + 16
    row_id = lax.broadcasted_iota(jnp.int32, (ey, nz), 0)
    lane_id = lax.broadcasted_iota(jnp.int32, (ey, nz), 1)
    cut_yl = (row_id == 8) & at_lower
    cut_yu = (row_id == 7 + ny) & at_upper
    cut_zl = lane_id == 0
    cut_zu = lane_id == nz - 1

    def up_y(v):
        return pltpu.roll(v, 1, axis=0)

    def down_y(v):
        return pltpu.roll(v, v.shape[0] - 1, axis=0)

    def z_sides(v):
        e, o = v[:, :half], v[:, half:]
        lower = jnp.concatenate([pltpu.roll(o, 1, axis=1), e], axis=1)
        upper = jnp.concatenate([o, pltpu.roll(e, half - 1, axis=1)], axis=1)
        return lower, upper

    def fine_weights(i, carry):
        at = i + HALO_S - 2
        v = stiff[at]
        zl, zu = z_sides(v)
        w = [
            v + stiff[at - 1], v + stiff[at + 1], v + up_y(v), v + down_y(v),
            v + jnp.where(cut_zl, v, zl), v + jnp.where(cut_zu, v, zu),
        ]
        diag = w[0] + w[1] + w[2] + w[3] + w[4] + w[5] + mass_share * v
        inv = damping / diag
        cuts = [None, None, cut_yl, cut_yu, cut_zl, cut_zu]
        for k in range(6):
            a = w[k] * inv
            a_ref[k, i] = a if cuts[k] is None else jnp.where(cuts[k], 0.0, a)
        d_ref[i] = diag
        return carry

    lax.fori_loop(0, nx + 4, fine_weights, 0)

    cy = ey // 2
    ccut_row = lax.broadcasted_iota(jnp.int32, (cy, half), 0)
    ccut_lane = lax.broadcasted_iota(jnp.int32, (cy, half), 1)
    ccut_yl = (ccut_row == 4) & at_lower
    ccut_yu = (ccut_row == 3 + ny // 2) & at_upper
    ccut_zl = ccut_lane == 0
    ccut_zu = ccut_lane == half - 1
    ca_ref[...] = jnp.zeros_like(ca_ref)

    def coarse_weights(i, carry):
        def both(at):
            v = stiff[at]
            return v[:, :half], v[:, half:]
        rows = [both(2 * i + k) for k in range(4)]
        zs = [e + o for e, o in rows]
        even, odd = rows[1][0] + rows[2][0], rows[1][1] + rows[2][1]
        u = even + odd
        for k, v in enumerate([zs[0] + zs[1], zs[2] + zs[3], u, even, odd]):
            tmp[k] = v
        tmp[5] = u + up_y(u)
        tmp[6] = u + down_y(u)

        def lows(k):
            return tmp[k, pl.ds(0, cy, stride=2), :]

        def highs(k):
            return tmp[k, pl.ds(1, cy, stride=2), :]

        def sums(k):
            return lows(k) + highs(k)

        ve, vo = sums(3), sums(4)
        w = [
            sums(0), sums(1), lows(5), highs(6),
            ve + jnp.where(ccut_zl, ve, pltpu.roll(vo, 1, axis=1)),
            vo + jnp.where(ccut_zu, vo, pltpu.roll(ve, half - 1, axis=1)),
        ]
        diag = w[0] + w[1] + w[2] + w[3] + w[4] + w[5] + mass_share * sums(2)
        inv = damping / diag
        cuts = [None, None, ccut_yl, ccut_yu, ccut_zl, ccut_zu]
        for k in range(6):
            a = w[k] * inv
            a = a if cuts[k] is None else jnp.where(cuts[k], 0.0, a)
            ca_ref[k, i, pl.ds(4, cy), :] = a
        cd_ref[i, pl.ds(4, cy), :] = diag
        return carry

    lax.fori_loop(0, nx // 2 + 6, coarse_weights, 0)

    for cond, lo_f, lo_c in ((at_lower, 0, 0), (at_upper, 8 + ny, 8 + ny // 2)):
        @pl.when(cond)
        def _(lo_f=lo_f, lo_c=lo_c):
            def body(i, carry):
                for c in range(3):
                    fine[c, i, pl.ds(lo_f, 8), :] = jnp.zeros((8, nz), jnp.float32)
                return carry
            lax.fori_loop(0, nx + 2 * HALO_F, body, 0)

            def body_c(i, carry):
                for c in range(3):
                    coarse[0, c, i, pl.ds(lo_c, 8), :] = jnp.zeros((8, half), jnp.float32)
                return carry
            lax.fori_loop(0, nx // 2 + 2 * HALO_C, body_c, 0)

    fine_copies = [
        halo(fine.at[c], HALO_F, nx, ny, f_send.at[c], f_recv.at[c]) for c in range(3)
    ]
    coarse_copies = [
        halo(coarse.at[0, c], HALO_C, nx // 2, ny // 2, c_send.at[c], c_recv.at[c])
        for c in range(3)
    ]

    xy = nx * ny
    low_lanes = lax.broadcasted_iota(jnp.int32, (xy, half), 1) < half // 2
    for c in range(3):
        to_sib(0, c).wait_recv()
        total = acc[c] + srecv[0, c]
        for q in range(1, pairs):
            to_rem(q, c).wait_recv()
            total = total + rrecv[q - 1, c]
        first, second = total[:xy], total[xy:]
        even = jnp.where(low_lanes, first, pltpu.roll(second, half // 2, axis=1))
        odd = jnp.where(low_lanes, pltpu.roll(first, half // 2, axis=1), second)
        source = jnp.concatenate([even, odd], axis=1).reshape(nx, ny, nz)
        diag = d_ref[pl.ds(2, nx), pl.ds(8, ny), :]
        fine[c, pl.ds(HALO_F, nx), pl.ds(8, ny), :] = damping * source / diag
        start(fine_copies[c])

    def gathered(ref, at, weights, i):
        v = ref[at]
        zl, zu = z_sides(v)
        return v, (
            weights[0, i] * ref[at - 1] + weights[1, i] * ref[at + 1]
            + weights[2, i] * up_y(v) + weights[3, i] * down_y(v)
            + weights[4, i] * zl + weights[5, i] * zu
        )

    for c in range(3):
        finish(fine_copies[c])
        f0, f1 = fine.at[c], fine1.at[c]

        def second_sweep(i, carry):
            v, near = gathered(f0, i + 1, a_ref, i)
            f1[i] = v * (2.0 - damping) + near
            return carry

        lax.fori_loop(0, nx + 4, second_sweep, 0)

        def restrict(i, carry):
            parts = []
            for k in range(2):
                at = 2 * i + 2 + k
                v, near = gathered(f1, at, a_ref, at)
                parts.append((f0[at + 1] - damping * v + near) * d_ref[at])
            r = parts[0] + parts[1]
            tmp2[...] = r[:, :half] + r[:, half:]
            rc = tmp2[pl.ds(8, ny // 2, stride=2), :] + tmp2[pl.ds(9, ny // 2, stride=2), :]
            coarse[0, c, i + HALO_C, pl.ds(8, ny // 2), :] = (
                rc / cd_ref[i + 3, pl.ds(8, ny // 2), :]
            )
            return carry

        lax.fori_loop(0, nx // 2, restrict, 0)
        start(coarse_copies[c])

    def gathered_c(ref, at, i):
        v = ref[at]
        return v, (
            ca_ref[0, i] * ref[at - 1] + ca_ref[1, i] * ref[at + 1]
            + ca_ref[2, i] * up_y(v) + ca_ref[3, i] * down_y(v)
            + ca_ref[4, i] * pltpu.roll(v, 1, axis=1)
            + ca_ref[5, i] * pltpu.roll(v, half - 1, axis=1)
        )

    from_halves = as_bf16(wide_c == jnp.where(wide_r < half, 2 * wide_r, 2 * wide_r - (nz - 1)))
    cx = nx // 2
    for c in range(3):
        finish(coarse_copies[c])
        c1 = coarse.at[0, c]
        for sweep in range(3):
            old, new = coarse.at[sweep, c], coarse.at[sweep + 1, c]

            def coarse_sweep(i, carry):
                v, near = gathered_c(old, i + 1, i)
                new[i + 1] = c1[i + 1] + (1.0 - damping) * v + near
                return carry

            lax.fori_loop(sweep, cx + 6 - sweep, coarse_sweep, 0)
        c4 = coarse.at[3, c]
        f0, f1 = fine.at[c], fine1.at[c]

        def prolong(i, carry):
            v = c4[i + 3, pl.ds(4, cy), :]
            tmp2[pl.ds(0, cy, stride=2), :] = v
            tmp2[pl.ds(1, cy, stride=2), :] = v
            w = tmp2[...]
            w = jnp.concatenate([w, w], axis=1)
            f1[2 * i] = f1[2 * i] + w
            f1[2 * i + 1] = f1[2 * i + 1] + w
            return carry

        lax.fori_loop(0, cx + 2, prolong, 0)

        def post1(i, carry):
            v, near = gathered(f1, i + 1, a_ref, i + 1)
            own_s[i] = f0[i + 2] + (1.0 - damping) * v + near
            return carry

        lax.fori_loop(0, nx + 2, post1, 0)

        def post2(i, carry):
            v, near = gathered(own_s, i + 1, a_ref, i + 2)
            r = (f0[i + 3] + (1.0 - damping) * v + near)[8:8 + ny]
            high, low = split2(r)
            out_ref[c, i] = dot(high, from_halves) + dot(low, from_halves)
            return carry

        lax.fori_loop(0, nx, post2, 0)

    for c in range(3):
        for q in range(pairs):
            to_sib(q, c).wait_send()
        for q in range(1, pairs):
            to_rem(q, c).wait_send()


def shards(mesh, grad_rows, dest_rank, dest_block, cell_class, class_stiffness):
    nx, ny, nz = cell_class.shape
    half = nz // 2
    passages, spans = mesh.shape["passage"], mesh.shape["span"]
    pairs = spans // 2
    nrows = grad_rows.shape[0]
    blocks = nx * ny * 2
    key = dest_rank[:, 0] * blocks + (dest_block % 2) * (blocks // 2) + dest_block // 2
    rows = grad_rows.transpose(1, 0, 2)
    vmem = pl.BlockSpec(memory_space=pltpu.VMEM)
    f32 = jnp.float32
    ey = ny + 16
    cx, ecy = nx // 2, ny // 2 + 16
    return pl.pallas_call(
        functools.partial(kernel, passages, spans),
        out_shape=jax.ShapeDtypeStruct((3, nx, ny, nz), f32),
        in_specs=[vmem, vmem, vmem, pl.BlockSpec(memory_space=pltpu.SMEM)],
        out_specs=vmem,
        scratch_shapes=[
            pltpu.VMEM((3, nrows, nz), jnp.bfloat16),
            pltpu.VMEM((pairs, 3, blocks, half), f32),
            pltpu.VMEM((pairs, 3, blocks, half), f32),
            pltpu.VMEM((pairs - 1, 3, blocks, half), f32),
            pltpu.VMEM((pairs - 1, 3, blocks, half), f32),
            pltpu.VMEM((3, blocks, half), f32),
            pltpu.VMEM((nx + 2 * HALO_S, ey, nz), f32),
            pltpu.VMEM((3, nx + 2 * HALO_F, ey, nz), f32),
            pltpu.VMEM((3, nx + 4, ey, nz), f32),
            pltpu.VMEM((4, 3, cx + 2 * HALO_C, ecy, half), f32),
            pltpu.VMEM((6, nx + 4, ey, nz), f32),
            pltpu.VMEM((nx + 4, ey, nz), f32),
            pltpu.VMEM((6, cx + 6, ecy, half), f32),
            pltpu.VMEM((cx + 6, ecy, half), f32),
            pltpu.VMEM((7, ey, half), f32),
            pltpu.VMEM((ey, half), f32),
            pltpu.VMEM((nx + 2, ey, nz), f32),
            pltpu.SemaphoreType.DMA((pairs, 3)),
            pltpu.SemaphoreType.DMA((pairs, 3)),
            pltpu.SemaphoreType.DMA((pairs - 1, 3)),
            pltpu.SemaphoreType.DMA((pairs - 1, 3)),
            pltpu.SemaphoreType.DMA((8,)),
            pltpu.SemaphoreType.DMA((8,)),
            pltpu.SemaphoreType.DMA((3, 8)),
            pltpu.SemaphoreType.DMA((3, 8)),
            pltpu.SemaphoreType.DMA((3, 8)),
            pltpu.SemaphoreType.DMA((3, 8)),
        ],
        compiler_params=pltpu.CompilerParams(
            collective_id=0, has_side_effects=True, vmem_limit_bytes=48 * 1024 * 1024
        ),
    )(key[None, :], rows, cell_class, class_stiffness[None, :])


def solution(mesh):
    placed = (
        P(("passage", "span"), None, None),
        P(("passage", "span"), None),
        P(("passage", "span")),
        P("passage", "span", None),
        P(),
    )
    return jax.shard_map(
        functools.partial(shards, mesh),
        mesh=mesh,
        in_specs=placed,
        out_specs=P(None, "passage", "span", None),
        check_vma=False,
    )
```

```python
import functools

import jax
import jax.numpy as jnp
from jax import lax
from jax.experimental import pallas as pl
from jax.experimental.pallas import tpu as pltpu
from jax.sharding import PartitionSpec as P

damping = 0.8
mass_share = 0.02
HALO_S = 7
HALO_F = 3
HALO_C = 4
DIRS = [(dx, dy) for dx in (-1, 0, 1) for dy in (-1, 0, 1) if (dx, dy) != (0, 0)]
MESH = pl.DeviceIdType.MESH


def split2(values):
    high = values.astype(jnp.bfloat16)
    low = (values - high.astype(jnp.float32)).astype(jnp.bfloat16)
    return high, low


def dot(a, b):
    return jnp.dot(a, b, preferred_element_type=jnp.float32)


def unrolled(low, high, body):
    for i in range(low, high):
        body(i, 0)


def as_bf16(mask):
    return jnp.where(mask, 1.0, 0.0).astype(jnp.bfloat16)


def kernel(
    passages, spans, key_hbm, rows_hbm, class_hbm, table_ref, out_ref,
    key_ref, rows_ref, class_ref, in_sem,
    split_ref, psend, srecv, rsend, rrecv, acc, stiff, fine, fine1, coarse,
    a_ref, d_ref, ca_ref, cd_ref, tmp, tmp2, own_s,
    sib_send, sib_recv, rem_send, rem_recv,
    st_send, st_recv, f_send, f_recv, c_send, c_recv,
):
    nx, ny, nz = class_ref.shape
    half = nz // 2
    blocks = nx * ny * 2
    nrows = rows_ref.shape[1]
    pairs = spans // 2
    p = lax.axis_index("passage")
    s = lax.axis_index("span")
    pair = s // 2
    core = s % 2
    sib = pair * 2 + 1 - core
    at_lower = s == 0
    at_upper = s == spans - 1

    def side(dx):
        return lax.rem(p + dx + passages, passages)

    def inside(dy):
        if dy == 0:
            return None
        return s + dy < spans if dy > 0 else s + dy >= 0

    def guarded(cond, action):
        if cond is None:
            action()
        else:
            pl.when(cond)(action)

    barrier = pltpu.get_barrier_semaphore()
    for dx, dy in DIRS:
        def greet(dx=dx, dy=dy):
            pl.semaphore_signal(barrier, inc=1, device_id=(side(dx), s + dy), device_id_type=MESH)
        guarded(inside(dy), greet)
    pl.semaphore_signal(barrier, inc=1, device_id=(p, sib), device_id_type=MESH)
    for q in range(1, pairs):
        pl.semaphore_signal(
            barrier, inc=1, device_id=(p, lax.rem(pair + q, pairs) * 2 + core), device_id_type=MESH
        )

    class_copy = pltpu.make_async_copy(class_hbm, class_ref, in_sem.at[0])
    class_copy.start()
    rows_copies = [
        pltpu.make_async_copy(rows_hbm.at[c], rows_ref.at[c], in_sem.at[1 + c]) for c in range(3)
    ]
    for copy in rows_copies:
        copy.start()
    key_copy = pltpu.make_async_copy(key_hbm, key_ref, in_sem.at[4])
    key_copy.start()

    def halo(buffer, halo_x, own_x, own_y, corner, send, recv):
        def spans_of(d, width, own, step):
            if d == 0:
                return (width, width, own)
            if d > 0:
                return (own + width - step, width - step, step)
            return (width, width + own, step)

        copies = []
        for k, (dx, dy) in enumerate(DIRS):
            sx, tx, lx = spans_of(dx, halo_x, own_x, halo_x if dy == 0 else corner)
            sy, ty, ly = spans_of(dy, 8, own_y, 8)
            copies.append(
                (dy, pltpu.make_async_remote_copy(
                    src_ref=buffer.at[pl.ds(sx, lx), pl.ds(sy, ly), :],
                    dst_ref=buffer.at[pl.ds(tx, lx), pl.ds(ty, ly), :],
                    send_sem=send.at[k],
                    recv_sem=recv.at[k],
                    device_id=(side(dx), s + dy),
                    device_id_type=MESH,
                ))
            )
        return copies

    def start(copies):
        for dy, copy in copies:
            guarded(inside(dy), copy.start)

    def finish(copies):
        for dy, copy in copies:
            guarded(inside(-dy), copy.wait_recv)
            guarded(inside(dy), copy.wait_send)

    wide_r = lax.broadcasted_iota(jnp.int32, (nz, nz), 0)
    wide_c = lax.broadcasted_iota(jnp.int32, (nz, nz), 1)
    to_halves = as_bf16(wide_r == jnp.where(wide_c < half, 2 * wide_c, 2 * wide_c - (nz - 1)))
    class_copy.wait()
    classes = class_ref[...].reshape(nx * ny, nz).astype(jnp.float32).astype(jnp.bfloat16)
    classes = dot(classes, to_halves)
    values = jnp.zeros_like(classes)
    for k in range(table_ref.shape[1]):
        values = jnp.where(classes == float(k), table_ref[0, k], values)
    stiff[pl.ds(HALO_S, nx), pl.ds(8, ny), :] = values.reshape(nx, ny, nz)

    in_r, in_c = wide_r % half, wide_c % half
    rows_perm = as_bf16(
        (wide_r // half == wide_c // half)
        & (in_r == jnp.where(in_c < half // 2, 2 * in_c, 2 * in_c - (half - 1)))
    )
    for c in range(3):
        rows_copies[c].wait()
        high, low = split2(rows_ref[c])
        parts = jnp.concatenate([high, low], axis=1)
        split_ref[c] = dot(parts, rows_perm).astype(jnp.bfloat16)

    block_iota = lax.broadcasted_iota(jnp.int32, (blocks, nrows), 0)
    key_copy.wait()
    key = key_ref[...]

    def chosen(target):
        return as_bf16(block_iota + target * blocks == key)

    def partial(hot, c):
        both = dot(hot, split_ref[c])
        return both[:, :half] + both[:, half:]

    n_greet = 3 * 2 + 2 + 1 + (pairs - 1)
    missing = 3 * (jnp.where(at_lower, 1, 0) + jnp.where(at_upper, 1, 0))
    pl.semaphore_wait(barrier, n_greet - missing)

    stiff_copies = halo(stiff, HALO_S, nx, ny, HALO_S, st_send, st_recv)
    start(stiff_copies)

    def to_sib(q, c):
        return pltpu.make_async_remote_copy(
            src_ref=psend.at[q, c], dst_ref=srecv.at[q, c],
            send_sem=sib_send.at[q, c], recv_sem=sib_recv.at[q, c],
            device_id=(p, sib), device_id_type=MESH,
        )

    def to_rem(q, c):
        return pltpu.make_async_remote_copy(
            src_ref=rsend.at[q - 1, c], dst_ref=rrecv.at[q - 1, c],
            send_sem=rem_send.at[q - 1, c], recv_sem=rem_recv.at[q - 1, c],
            device_id=(p, lax.rem(pair + q, pairs) * 2 + core), device_id_type=MESH,
        )

    for q in list(range(1, pairs)):
        target = lax.rem(pair + q, pairs) * 2
        hot = chosen(target + 1 - core)
        for c in range(3):
            psend[q, c] = partial(hot, c)
            to_sib(q, c).start()
    for q in range(1, pairs):
        target = lax.rem(pair + q, pairs) * 2
        hot = chosen(target + core)
        for c in range(3):
            own = partial(hot, c)
            to_sib(q, c).wait_recv()
            rsend[q - 1, c] = own + srecv[q, c]
            to_rem(q, c).start()
    hot = chosen(pair * 2 + 1 - core)
    for c in range(3):
        psend[0, c] = partial(hot, c)
        to_sib(0, c).start()
    hot = chosen(s)
    for c in range(3):
        acc[c] = partial(hot, c)

    finish(stiff_copies)
    total_x = nx + 2 * HALO_S

    @pl.when(at_lower)
    def _():
        def body(i, carry):
            stiff[i, pl.ds(0, 8), :] = jnp.broadcast_to(stiff[i, pl.ds(8, 1), :], (8, nz))
            return carry
        lax.fori_loop(0, total_x, body, 0)

    @pl.when(at_upper)
    def _():
        def body(i, carry):
            stiff[i, pl.ds(8 + ny, 8), :] = jnp.broadcast_to(
                stiff[i, pl.ds(7 + ny, 1), :], (8, nz)
            )
            return carry
        lax.fori_loop(0, total_x, body, 0)

    ey = ny + 16
    row_id = lax.broadcasted_iota(jnp.int32, (ey, nz), 0)
    lane_id = lax.broadcasted_iota(jnp.int32, (ey, nz), 1)
    cut_yl = (row_id == 8) & at_lower
    cut_yu = (row_id == 7 + ny) & at_upper
    cut_zl = lane_id == 0
    cut_zu = lane_id == nz - 1

    def up_y(v):
        return pltpu.roll(v, 1, axis=0)

    def down_y(v):
        return pltpu.roll(v, v.shape[0] - 1, axis=0)

    def z_sides(v):
        e, o = v[:, :half], v[:, half:]
        lower = jnp.concatenate([pltpu.roll(o, 1, axis=1), e], axis=1)
        upper = jnp.concatenate([o, pltpu.roll(e, half - 1, axis=1)], axis=1)
        return lower, upper

    def fine_weights(i, carry):
        at = i + HALO_S - 2
        v = stiff[at]
        zl, zu = z_sides(v)
        w = [
            v + stiff[at - 1], v + stiff[at + 1], v + up_y(v), v + down_y(v),
            v + jnp.where(cut_zl, v, zl), v + jnp.where(cut_zu, v, zu),
        ]
        diag = w[0] + w[1] + w[2] + w[3] + w[4] + w[5] + mass_share * v
        inv = damping / diag
        cuts = [None, None, cut_yl, cut_yu, cut_zl, cut_zu]
        for k in range(6):
            a = w[k] * inv
            a_ref[k, i] = a if cuts[k] is None else jnp.where(cuts[k], 0.0, a)
        d_ref[i] = diag
        return carry

    lax.fori_loop(0, nx + 4, fine_weights, 0, unroll=2)

    cy = ey // 2
    ccut_row = lax.broadcasted_iota(jnp.int32, (cy, half), 0)
    ccut_lane = lax.broadcasted_iota(jnp.int32, (cy, half), 1)
    ccut_yl = (ccut_row == 4) & at_lower
    ccut_yu = (ccut_row == 3 + ny // 2) & at_upper
    ccut_zl = ccut_lane == 0
    ccut_zu = ccut_lane == half - 1
    ca_ref[...] = jnp.zeros_like(ca_ref)

    def coarse_weights(i, carry):
        def both(at):
            v = stiff[at]
            return v[:, :half], v[:, half:]
        rows = [both(2 * i + k) for k in range(4)]
        zs = [e + o for e, o in rows]
        even, odd = rows[1][0] + rows[2][0], rows[1][1] + rows[2][1]
        u = even + odd
        for k, v in enumerate([zs[0] + zs[1], zs[2] + zs[3], u, even, odd]):
            tmp[k] = v
        tmp[5] = u + up_y(u)
        tmp[6] = u + down_y(u)

        def lows(k):
            return tmp[k, pl.ds(0, cy, stride=2), :]

        def highs(k):
            return tmp[k, pl.ds(1, cy, stride=2), :]

        def sums(k):
            return lows(k) + highs(k)

        ve, vo = sums(3), sums(4)
        w = [
            sums(0), sums(1), lows(5), highs(6),
            ve + jnp.where(ccut_zl, ve, pltpu.roll(vo, 1, axis=1)),
            vo + jnp.where(ccut_zu, vo, pltpu.roll(ve, half - 1, axis=1)),
        ]
        diag = w[0] + w[1] + w[2] + w[3] + w[4] + w[5] + mass_share * sums(2)
        inv = damping / diag
        cuts = [None, None, ccut_yl, ccut_yu, ccut_zl, ccut_zu]
        for k in range(6):
            a = w[k] * inv
            a = a if cuts[k] is None else jnp.where(cuts[k], 0.0, a)
            ca_ref[k, i, pl.ds(4, cy), :] = a
        cd_ref[i, pl.ds(4, cy), :] = diag
        return carry

    lax.fori_loop(0, nx // 2 + 6, coarse_weights, 0, unroll=2)

    for cond, lo_f, lo_c in ((at_lower, 0, 0), (at_upper, 8 + ny, 8 + ny // 2)):
        @pl.when(cond)
        def _(lo_f=lo_f, lo_c=lo_c):
            def body(i, carry):
                for c in range(3):
                    fine[c, i, pl.ds(lo_f, 8), :] = jnp.zeros((8, nz), jnp.float32)
                return carry
            lax.fori_loop(0, nx + 2 * HALO_F, body, 0)

            def body_c(i, carry):
                for c in range(3):
                    coarse[0, c, i, pl.ds(lo_c, 8), :] = jnp.zeros((8, half), jnp.float32)
                return carry
            lax.fori_loop(0, nx // 2 + 2 * HALO_C, body_c, 0)

    for c in range(3):
        for at in (0, nx + 2 * HALO_F - 1):
            for lo in (0, 8 + ny):
                fine[c, at, pl.ds(lo, 8), :] = jnp.zeros((8, nz), jnp.float32)

    fine_copies = [
        halo(fine.at[c], HALO_F, nx, ny, HALO_F - 1, f_send.at[c], f_recv.at[c]) for c in range(3)
    ]
    coarse_copies = [
        halo(coarse.at[0, c], HALO_C, nx // 2, ny // 2, HALO_C, c_send.at[c], c_recv.at[c])
        for c in range(3)
    ]

    xy = nx * ny
    low_lanes = lax.broadcasted_iota(jnp.int32, (xy, half), 1) < half // 2
    for c in range(3):
        to_sib(0, c).wait_recv()
        total = acc[c] + srecv[0, c]
        for q in range(1, pairs):
            to_rem(q, c).wait_recv()
            total = total + rrecv[q - 1, c]
        first, second = total[:xy], total[xy:]
        even = jnp.where(low_lanes, first, pltpu.roll(second, half // 2, axis=1))
        odd = jnp.where(low_lanes, pltpu.roll(first, half // 2, axis=1), second)
        source = jnp.concatenate([even, odd], axis=1).reshape(nx, ny, nz)
        diag = d_ref[pl.ds(2, nx), pl.ds(8, ny), :]
        fine[c, pl.ds(HALO_F, nx), pl.ds(8, ny), :] = damping * source / diag
        start(fine_copies[c])

    def gathered(ref, at, weights, i):
        v = ref[at]
        zl, zu = z_sides(v)
        return v, (
            weights[0, i] * ref[at - 1] + weights[1, i] * ref[at + 1]
            + weights[2, i] * up_y(v) + weights[3, i] * down_y(v)
            + weights[4, i] * zl + weights[5, i] * zu
        )

    for c in range(3):
        finish(fine_copies[c])
        f0, f1 = fine.at[c], fine1.at[c]

        def second_sweep(i, carry):
            v, near = gathered(f0, i + 1, a_ref, i)
            f1[i] = v * (2.0 - damping) + near
            return carry

        unrolled(0, nx + 4, second_sweep)

        def restrict(i, carry):
            parts = []
            for k in range(2):
                at = 2 * i + 2 + k
                v, near = gathered(f1, at, a_ref, at)
                parts.append((f0[at + 1] - damping * v + near) * d_ref[at])
            r = parts[0] + parts[1]
            r = r[8:8 + ny]
            tmp2[pl.ds(8, ny), :] = r[:, :half] + r[:, half:]
            rc = tmp2[pl.ds(8, ny // 2, stride=2), :] + tmp2[pl.ds(9, ny // 2, stride=2), :]
            coarse[0, c, i + HALO_C, pl.ds(8, ny // 2), :] = (
                rc / cd_ref[i + 3, pl.ds(8, ny // 2), :]
            )
            return carry

        unrolled(0, nx // 2, restrict)
        start(coarse_copies[c])

    def gathered_c(ref, at, i):
        v = ref[at]
        return v, (
            ca_ref[0, i] * ref[at - 1] + ca_ref[1, i] * ref[at + 1]
            + ca_ref[2, i] * up_y(v) + ca_ref[3, i] * down_y(v)
            + ca_ref[4, i] * pltpu.roll(v, 1, axis=1)
            + ca_ref[5, i] * pltpu.roll(v, half - 1, axis=1)
        )

    from_halves = as_bf16(wide_c == jnp.where(wide_r < half, 2 * wide_r, 2 * wide_r - (nz - 1)))
    cx = nx // 2
    for c in range(3):
        finish(coarse_copies[c])
        c1 = coarse.at[0, c]
        for sweep in range(3):
            old, new = coarse.at[sweep, c], coarse.at[sweep + 1, c]

            def coarse_sweep(i, carry):
                v, near = gathered_c(old, i + 1, i)
                new[i + 1] = c1[i + 1] + (1.0 - damping) * v + near
                return carry

            unrolled(sweep, cx + 6 - sweep, coarse_sweep)
        c4 = coarse.at[3, c]
        f0, f1 = fine.at[c], fine1.at[c]

        def prolong(i, carry):
            v = c4[i + 3, pl.ds(4, cy), :]
            tmp2[pl.ds(0, cy, stride=2), :] = v
            tmp2[pl.ds(1, cy, stride=2), :] = v
            w = tmp2[...]
            w = jnp.concatenate([w, w], axis=1)
            f1[2 * i] = f1[2 * i] + w
            f1[2 * i + 1] = f1[2 * i + 1] + w
            return carry

        unrolled(0, cx + 2, prolong)

        def post1(i, carry):
            v, near = gathered(f1, i + 1, a_ref, i + 1)
            own_s[i] = f0[i + 2] + (1.0 - damping) * v + near
            return carry

        unrolled(0, nx + 2, post1)

        def post2(i, carry):
            v, near = gathered(own_s, i + 1, a_ref, i + 2)
            r = (f0[i + 3] + (1.0 - damping) * v + near)[8:8 + ny]
            high, low = split2(r)
            out_ref[c, i] = dot(high, from_halves) + dot(low, from_halves)
            return carry

        unrolled(0, nx, post2)

    for c in range(3):
        for q in range(pairs):
            to_sib(q, c).wait_send()
        for q in range(1, pairs):
            to_rem(q, c).wait_send()


def shards(mesh, grad_rows, dest_rank, dest_block, cell_class, class_stiffness):
    nx, ny, nz = cell_class.shape
    half = nz // 2
    passages, spans = mesh.shape["passage"], mesh.shape["span"]
    pairs = spans // 2
    nrows = grad_rows.shape[0]
    blocks = nx * ny * 2
    key = dest_rank[:, 0] * blocks + (dest_block % 2) * (blocks // 2) + dest_block // 2
    rows = grad_rows.transpose(1, 0, 2)
    vmem = pl.BlockSpec(memory_space=pltpu.VMEM)
    hbm = pl.BlockSpec(memory_space=pl.ANY)
    f32 = jnp.float32
    ey = ny + 16
    cx, ecy = nx // 2, ny // 2 + 16
    return pl.pallas_call(
        functools.partial(kernel, passages, spans),
        out_shape=jax.ShapeDtypeStruct((3, nx, ny, nz), f32),
        in_specs=[hbm, hbm, hbm, pl.BlockSpec(memory_space=pltpu.SMEM)],
        out_specs=vmem,
        scratch_shapes=[
            pltpu.VMEM((1, nrows), jnp.int32),
            pltpu.VMEM((3, nrows, half), f32),
            pltpu.VMEM((nx, ny, nz), jnp.int32),
            pltpu.SemaphoreType.DMA((5,)),
            pltpu.VMEM((3, nrows, nz), jnp.bfloat16),
            pltpu.VMEM((pairs, 3, blocks, half), f32),
            pltpu.VMEM((pairs, 3, blocks, half), f32),
            pltpu.VMEM((pairs - 1, 3, blocks, half), f32),
            pltpu.VMEM((pairs - 1, 3, blocks, half), f32),
            pltpu.VMEM((3, blocks, half), f32),
            pltpu.VMEM((nx + 2 * HALO_S, ey, nz), f32),
            pltpu.VMEM((3, nx + 2 * HALO_F, ey, nz), f32),
            pltpu.VMEM((3, nx + 4, ey, nz), f32),
            pltpu.VMEM((4, 3, cx + 2 * HALO_C, ecy, half), f32),
            pltpu.VMEM((6, nx + 4, ey, nz), f32),
            pltpu.VMEM((nx + 4, ey, nz), f32),
            pltpu.VMEM((6, cx + 6, ecy, half), f32),
            pltpu.VMEM((cx + 6, ecy, half), f32),
            pltpu.VMEM((7, ey, half), f32),
            pltpu.VMEM((ey, half), f32),
            pltpu.VMEM((nx + 2, ey, nz), f32),
            pltpu.SemaphoreType.DMA((pairs, 3)),
            pltpu.SemaphoreType.DMA((pairs, 3)),
            pltpu.SemaphoreType.DMA((pairs - 1, 3)),
            pltpu.SemaphoreType.DMA((pairs - 1, 3)),
            pltpu.SemaphoreType.DMA((8,)),
            pltpu.SemaphoreType.DMA((8,)),
            pltpu.SemaphoreType.DMA((3, 8)),
            pltpu.SemaphoreType.DMA((3, 8)),
            pltpu.SemaphoreType.DMA((3, 8)),
            pltpu.SemaphoreType.DMA((3, 8)),
        ],
        compiler_params=pltpu.CompilerParams(
            collective_id=0, has_side_effects=True, vmem_limit_bytes=60 * 1024 * 1024
        ),
    )(key[None, :], rows, cell_class, class_stiffness[None, :])


def solution(mesh):
    placed = (
        P(("passage", "span"), None, None),
        P(("passage", "span"), None),
        P(("passage", "span")),
        P("passage", "span", None),
        P(),
    )
    return jax.shard_map(
        functools.partial(shards, mesh),
        mesh=mesh,
        in_specs=placed,
        out_specs=P(None, "passage", "span", None),
        check_vma=False,
    )
```

```python
import functools

import jax
import jax.numpy as jnp
from jax import lax
from jax.experimental import pallas as pl
from jax.experimental.pallas import tpu as pltpu
from jax.sharding import PartitionSpec as P

damping = 0.8
mass_share = 0.02
HALO_S = 7
HALO_F = 3
HALO_C = 4
DIRS = [(-1, 0), (1, 0), (0, -1), (0, 1)]
CORNERS = [(dx, dy) for dx in (-1, 1) for dy in (-1, 1)]
MESH = pl.DeviceIdType.MESH


def split2(values):
    high = values.astype(jnp.bfloat16)
    low = (values - high.astype(jnp.float32)).astype(jnp.bfloat16)
    return high, low


def dot(a, b):
    return jnp.dot(a, b, preferred_element_type=jnp.float32)


def unrolled(low, high, body):
    for i in range(low, high):
        body(i, 0)


def as_bf16(mask):
    return jnp.where(mask, 1.0, 0.0).astype(jnp.bfloat16)


def kernel(
    passages, spans, key_hbm, rows_hbm, class_hbm, table_ref, out_ref,
    key_ref, rows_ref, class_ref, in_sem,
    split_ref, psend, srecv, rsend, rrecv, acc, stiff, fine, fine1, coarse,
    inv_d, a_ref, d_ref, ca_ref, cd_ref, tmp, tmp2, own_s,
    sib_send, sib_recv, rem_send, rem_recv,
    st_send, st_recv, f_send, f_recv, c_send, c_recv,
):
    nx, ny, nz = class_ref.shape
    half = nz // 2
    blocks = nx * ny * 2
    nrows = rows_ref.shape[1]
    pairs = spans // 2
    p = lax.axis_index("passage")
    s = lax.axis_index("span")
    pair = s // 2
    core = s % 2
    sib = pair * 2 + 1 - core
    at_lower = s == 0
    at_upper = s == spans - 1

    def side(dx):
        return lax.rem(p + dx + passages, passages)

    def inside(dy):
        if dy == 0:
            return None
        return s + dy < spans if dy > 0 else s + dy >= 0

    def guarded(cond, action):
        if cond is None:
            action()
        else:
            pl.when(cond)(action)

    barrier = pltpu.get_barrier_semaphore()
    for dx, dy in DIRS:
        def greet(dx=dx, dy=dy):
            pl.semaphore_signal(barrier, inc=1, device_id=(side(dx), s + dy), device_id_type=MESH)
        guarded(inside(dy), greet)
    pl.semaphore_signal(barrier, inc=1, device_id=(p, sib), device_id_type=MESH)
    for q in range(1, pairs):
        pl.semaphore_signal(
            barrier, inc=1, device_id=(p, lax.rem(pair + q, pairs) * 2 + core), device_id_type=MESH
        )

    class_copy = pltpu.make_async_copy(class_hbm, class_ref, in_sem.at[0])
    class_copy.start()
    rows_copies = [
        pltpu.make_async_copy(rows_hbm.at[c], rows_ref.at[c], in_sem.at[1 + c]) for c in range(3)
    ]
    for copy in rows_copies:
        copy.start()
    key_copy = pltpu.make_async_copy(key_hbm, key_ref, in_sem.at[4])
    key_copy.start()

    def halo(buffer, halo_x, own_x, own_y, corner, send, recv):
        def copy(k, target, sx, tx, lx, sy, ty, ly):
            return pltpu.make_async_remote_copy(
                src_ref=buffer.at[pl.ds(sx, lx), pl.ds(sy, ly), :],
                dst_ref=buffer.at[pl.ds(tx, lx), pl.ds(ty, ly), :],
                send_sem=send.at[k],
                recv_sem=recv.at[k],
                device_id=target,
                device_id_type=MESH,
            )

        def along_y(dy):
            return (own_y, 0, 8) if dy > 0 else (8, 8 + own_y, 8)

        first, second = [], []
        for k, (dx, dy) in enumerate(DIRS):
            if dx:
                strip = (own_x, 0, halo_x) if dx > 0 else (halo_x, halo_x + own_x, halo_x)
                rows = (8, 8, own_y)
            else:
                strip, rows = (halo_x, halo_x, own_x), along_y(dy)
            first.append((dy, copy(k, (side(dx), s + dy), *strip, *rows)))
        for k, (dx, dy) in enumerate(CORNERS):
            at = halo_x - corner if dx < 0 else halo_x + own_x
            second.append((dy, copy(4 + k, (p, s + dy), at, at, corner, *along_y(dy))))
        return first, second

    def start(copies):
        for dy, copy in copies:
            guarded(inside(dy), copy.start)

    def arrive(copies):
        for dy, copy in copies:
            guarded(inside(-dy), copy.wait_recv)

    def sent(copies):
        for dy, copy in copies:
            guarded(inside(dy), copy.wait_send)

    wide_r = lax.broadcasted_iota(jnp.int32, (nz, nz), 0)
    wide_c = lax.broadcasted_iota(jnp.int32, (nz, nz), 1)
    to_halves = as_bf16(wide_r == jnp.where(wide_c < half, 2 * wide_c, 2 * wide_c - (nz - 1)))
    class_copy.wait()
    classes = class_ref[...].reshape(nx * ny, nz).astype(jnp.float32).astype(jnp.bfloat16)
    classes = dot(classes, to_halves)
    values = jnp.zeros_like(classes)
    for k in range(table_ref.shape[1]):
        values = jnp.where(classes == float(k), table_ref[0, k], values)
    stiff[pl.ds(HALO_S, nx), pl.ds(8, ny), :] = values.reshape(nx, ny, nz)

    in_r, in_c = wide_r % half, wide_c % half
    rows_perm = as_bf16(
        (wide_r // half == wide_c // half)
        & (in_r == jnp.where(in_c < half // 2, 2 * in_c, 2 * in_c - (half - 1)))
    )
    for c in range(3):
        rows_copies[c].wait()
        high, low = split2(rows_ref[c])
        parts = jnp.concatenate([high, low], axis=1)
        split_ref[c] = dot(parts, rows_perm).astype(jnp.bfloat16)

    block_iota = lax.broadcasted_iota(jnp.int32, (blocks, nrows), 0)
    key_copy.wait()
    key = key_ref[...]

    def chosen(target):
        return as_bf16(block_iota + target * blocks == key)

    def partial(hot, c):
        both = dot(hot, split_ref[c])
        return both[:, :half] + both[:, half:]

    n_greet = 2 + 2 + 1 + (pairs - 1)
    missing = (jnp.where(at_lower, 1, 0) + jnp.where(at_upper, 1, 0))
    pl.semaphore_wait(barrier, n_greet - missing)

    stiff_first, stiff_second = halo(stiff, HALO_S, nx, ny, HALO_S, st_send, st_recv)
    start(stiff_first)

    def to_sib(q, c):
        return pltpu.make_async_remote_copy(
            src_ref=psend.at[q, c], dst_ref=srecv.at[q, c],
            send_sem=sib_send.at[q, c], recv_sem=sib_recv.at[q, c],
            device_id=(p, sib), device_id_type=MESH,
        )

    def to_rem(q, c):
        return pltpu.make_async_remote_copy(
            src_ref=rsend.at[q - 1, c], dst_ref=rrecv.at[q - 1, c],
            send_sem=rem_send.at[q - 1, c], recv_sem=rem_recv.at[q - 1, c],
            device_id=(p, lax.rem(pair + q, pairs) * 2 + core), device_id_type=MESH,
        )

    for q in list(range(1, pairs)):
        target = lax.rem(pair + q, pairs) * 2
        hot = chosen(target + 1 - core)
        for c in range(3):
            psend[q, c] = partial(hot, c)
            to_sib(q, c).start()
    for q in range(1, pairs):
        target = lax.rem(pair + q, pairs) * 2
        hot = chosen(target + core)
        for c in range(3):
            own = partial(hot, c)
            to_sib(q, c).wait_recv()
            rsend[q - 1, c] = own + srecv[q, c]
            to_rem(q, c).start()
    hot = chosen(pair * 2 + 1 - core)
    for c in range(3):
        psend[0, c] = partial(hot, c)
        to_sib(0, c).start()
    hot = chosen(s)
    for c in range(3):
        acc[c] = partial(hot, c)

    arrive(stiff_first)
    start(stiff_second)
    total_x = nx + 2 * HALO_S

    @pl.when(at_lower)
    def _():
        def body(i, carry):
            stiff[i, pl.ds(0, 8), :] = jnp.broadcast_to(stiff[i, pl.ds(8, 1), :], (8, nz))
            return carry
        lax.fori_loop(0, total_x, body, 0)

    @pl.when(at_upper)
    def _():
        def body(i, carry):
            stiff[i, pl.ds(8 + ny, 8), :] = jnp.broadcast_to(
                stiff[i, pl.ds(7 + ny, 1), :], (8, nz)
            )
            return carry
        lax.fori_loop(0, total_x, body, 0)

    ey = ny + 16
    row_id = lax.broadcasted_iota(jnp.int32, (ey, nz), 0)
    lane_id = lax.broadcasted_iota(jnp.int32, (ey, nz), 1)
    cut_yl = (row_id == 8) & at_lower
    cut_yu = (row_id == 7 + ny) & at_upper
    cut_zl = lane_id == 0
    cut_zu = lane_id == nz - 1

    def up_y(v):
        return pltpu.roll(v, 1, axis=0)

    def down_y(v):
        return pltpu.roll(v, v.shape[0] - 1, axis=0)

    def z_sides(v):
        e, o = v[:, :half], v[:, half:]
        lower = jnp.concatenate([pltpu.roll(o, 1, axis=1), e], axis=1)
        upper = jnp.concatenate([o, pltpu.roll(e, half - 1, axis=1)], axis=1)
        return lower, upper

    def own_diagonal(i, carry):
        at = i + HALO_S
        v = stiff[at]
        zl, zu = z_sides(v)
        rows = pl.ds(8, ny)
        inner = v + up_y(v) + v + down_y(v)
        inner = inner + v + jnp.where(cut_zl, v, zl) + v + jnp.where(cut_zu, v, zu)
        inner = (inner + (2.0 + mass_share) * v)[8:8 + ny]
        inner = inner + stiff[at - 1, rows, :] + stiff[at + 1, rows, :]
        inv_d[i] = damping / inner
        return carry

    unrolled(0, nx, own_diagonal)

    def fine_weights(i, carry):
        at = i + HALO_S - 2
        v = stiff[at]
        zl, zu = z_sides(v)
        w = [
            v + stiff[at - 1], v + stiff[at + 1], v + up_y(v), v + down_y(v),
            v + jnp.where(cut_zl, v, zl), v + jnp.where(cut_zu, v, zu),
        ]
        diag = w[0] + w[1] + w[2] + w[3] + w[4] + w[5] + mass_share * v
        inv = damping / diag
        cuts = [None, None, cut_yl, cut_yu, cut_zl, cut_zu]
        for k in range(6):
            a = w[k] * inv
            a_ref[k, i] = a if cuts[k] is None else jnp.where(cuts[k], 0.0, a)
        d_ref[i] = diag
        return carry


    cy = ey // 2
    ccut_row = lax.broadcasted_iota(jnp.int32, (cy, half), 0)
    ccut_lane = lax.broadcasted_iota(jnp.int32, (cy, half), 1)
    ccut_yl = (ccut_row == 4) & at_lower
    ccut_yu = (ccut_row == 3 + ny // 2) & at_upper
    ccut_zl = ccut_lane == 0
    ccut_zu = ccut_lane == half - 1

    def coarse_weights(i, carry):
        def both(at):
            v = stiff[at]
            return v[:, :half], v[:, half:]
        rows = [both(2 * i + k) for k in range(4)]
        zs = [e + o for e, o in rows]
        even, odd = rows[1][0] + rows[2][0], rows[1][1] + rows[2][1]
        u = even + odd
        for k, v in enumerate([zs[0] + zs[1], zs[2] + zs[3], u, even, odd]):
            tmp[k] = v
        tmp[5] = u + up_y(u)
        tmp[6] = u + down_y(u)

        def lows(k):
            return tmp[k, pl.ds(0, cy, stride=2), :]

        def highs(k):
            return tmp[k, pl.ds(1, cy, stride=2), :]

        def sums(k):
            return lows(k) + highs(k)

        ve, vo = sums(3), sums(4)
        w = [
            sums(0), sums(1), lows(5), highs(6),
            ve + jnp.where(ccut_zl, ve, pltpu.roll(vo, 1, axis=1)),
            vo + jnp.where(ccut_zu, vo, pltpu.roll(ve, half - 1, axis=1)),
        ]
        diag = w[0] + w[1] + w[2] + w[3] + w[4] + w[5] + mass_share * sums(2)
        inv = damping / diag
        cuts = [None, None, ccut_yl, ccut_yu, ccut_zl, ccut_zu]
        for k in range(6):
            a = w[k] * inv
            a = a if cuts[k] is None else jnp.where(cuts[k], 0.0, a)
            ca_ref[k, i, pl.ds(4, cy), :] = a
        cd_ref[i, pl.ds(4, cy), :] = diag
        return carry


    for cond, lo_f, lo_c in ((at_lower, 0, 0), (at_upper, 8 + ny, 8 + ny // 2)):
        @pl.when(cond)
        def _(lo_f=lo_f, lo_c=lo_c):
            def body(i, carry):
                for c in range(3):
                    fine[c, i, pl.ds(lo_f, 8), :] = jnp.zeros((8, nz), jnp.float32)
                return carry
            lax.fori_loop(0, nx + 2 * HALO_F, body, 0)

            def body_c(i, carry):
                for c in range(3):
                    coarse[0, c, i, pl.ds(lo_c, 8), :] = jnp.zeros((8, half), jnp.float32)
                return carry
            lax.fori_loop(0, nx // 2 + 2 * HALO_C, body_c, 0)

    for c in range(3):
        for at in (0, nx + 2 * HALO_F - 1):
            for lo in (0, 8 + ny):
                fine[c, at, pl.ds(lo, 8), :] = jnp.zeros((8, nz), jnp.float32)

    fine_copies = [
        halo(fine.at[c], HALO_F, nx, ny, HALO_F - 1, f_send.at[c], f_recv.at[c]) for c in range(3)
    ]
    coarse_copies = [
        halo(coarse.at[0, c], HALO_C, nx // 2, ny // 2, HALO_C, c_send.at[c], c_recv.at[c])
        for c in range(3)
    ]

    xy = nx * ny
    low_lanes = lax.broadcasted_iota(jnp.int32, (xy, half), 1) < half // 2
    for c in range(3):
        to_sib(0, c).wait_recv()
        total = acc[c] + srecv[0, c]
        for q in range(1, pairs):
            to_rem(q, c).wait_recv()
            total = total + rrecv[q - 1, c]
        first, second = total[:xy], total[xy:]
        even = jnp.where(low_lanes, first, pltpu.roll(second, half // 2, axis=1))
        odd = jnp.where(low_lanes, pltpu.roll(first, half // 2, axis=1), second)
        source = jnp.concatenate([even, odd], axis=1).reshape(nx, ny, nz)
        fine[c, pl.ds(HALO_F, nx), pl.ds(8, ny), :] = source * inv_d[...]
        start(fine_copies[c][0])

    arrive(stiff_second)
    ca_ref[...] = jnp.zeros_like(ca_ref)
    lax.fori_loop(0, nx + 4, fine_weights, 0, unroll=2)
    lax.fori_loop(0, nx // 2 + 6, coarse_weights, 0, unroll=2)

    def gathered(ref, at, weights, i):
        v = ref[at]
        zl, zu = z_sides(v)
        return v, (
            weights[0, i] * ref[at - 1] + weights[1, i] * ref[at + 1]
            + weights[2, i] * up_y(v) + weights[3, i] * down_y(v)
            + weights[4, i] * zl + weights[5, i] * zu
        )

    def down(c):
        arrive(fine_copies[c][1])
        f0, f1 = fine.at[c], fine1.at[c]

        def second_sweep(i, carry):
            v, near = gathered(f0, i + 1, a_ref, i)
            f1[i] = v * (2.0 - damping) + near
            return carry

        unrolled(0, nx + 4, second_sweep)

        def restrict(i, carry):
            parts = []
            for k in range(2):
                at = 2 * i + 2 + k
                v, near = gathered(f1, at, a_ref, at)
                parts.append((f0[at + 1] - damping * v + near) * d_ref[at])
            r = parts[0] + parts[1]
            r = r[8:8 + ny]
            tmp2[pl.ds(8, ny), :] = r[:, :half] + r[:, half:]
            rc = tmp2[pl.ds(8, ny // 2, stride=2), :] + tmp2[pl.ds(9, ny // 2, stride=2), :]
            coarse[0, c, i + HALO_C, pl.ds(8, ny // 2), :] = (
                rc / cd_ref[i + 3, pl.ds(8, ny // 2), :]
            )
            return carry

        unrolled(0, nx // 2, restrict)
        start(coarse_copies[c][0])

    def gathered_c(ref, at, i):
        v = ref[at]
        return v, (
            ca_ref[0, i] * ref[at - 1] + ca_ref[1, i] * ref[at + 1]
            + ca_ref[2, i] * up_y(v) + ca_ref[3, i] * down_y(v)
            + ca_ref[4, i] * pltpu.roll(v, 1, axis=1)
            + ca_ref[5, i] * pltpu.roll(v, half - 1, axis=1)
        )

    from_halves = as_bf16(wide_c == jnp.where(wide_r < half, 2 * wide_r, 2 * wide_r - (nz - 1)))
    cx = nx // 2

    def back_up(c):
        arrive(coarse_copies[c][1])
        c1 = coarse.at[0, c]
        for sweep in range(3):
            old, new = coarse.at[sweep, c], coarse.at[sweep + 1, c]

            def coarse_sweep(i, carry):
                v, near = gathered_c(old, i + 1, i)
                new[i + 1] = c1[i + 1] + (1.0 - damping) * v + near
                return carry

            unrolled(sweep, cx + 6 - sweep, coarse_sweep)
        c4 = coarse.at[3, c]
        f0, f1 = fine.at[c], fine1.at[c]

        def prolong(i, carry):
            v = c4[i + 3, pl.ds(4, cy), :]
            tmp2[pl.ds(0, cy, stride=2), :] = v
            tmp2[pl.ds(1, cy, stride=2), :] = v
            w = tmp2[...]
            w = jnp.concatenate([w, w], axis=1)
            f1[2 * i] = f1[2 * i] + w
            f1[2 * i + 1] = f1[2 * i + 1] + w
            return carry

        unrolled(0, cx + 2, prolong)

        def post1(i, carry):
            v, near = gathered(f1, i + 1, a_ref, i + 1)
            own_s[i] = f0[i + 2] + (1.0 - damping) * v + near
            return carry

        unrolled(0, nx + 2, post1)

        def post2(i, carry):
            v, near = gathered(own_s, i + 1, a_ref, i + 2)
            r = (f0[i + 3] + (1.0 - damping) * v + near)[8:8 + ny]
            high, low = split2(r)
            out_ref[c, i] = dot(high, from_halves) + dot(low, from_halves)
            return carry

        unrolled(0, nx, post2)

    for copies, work in ((fine_copies, down), (coarse_copies, back_up)):
        for c in range(4):
            if c < 3:
                arrive(copies[c][0])
                start(copies[c][1])
            if c > 0:
                work(c - 1)

    for first, second in [(stiff_first, stiff_second)] + fine_copies + coarse_copies:
        sent(first)
        sent(second)
    for c in range(3):
        for q in range(pairs):
            to_sib(q, c).wait_send()
        for q in range(1, pairs):
            to_rem(q, c).wait_send()


def shards(mesh, grad_rows, dest_rank, dest_block, cell_class, class_stiffness):
    nx, ny, nz = cell_class.shape
    half = nz // 2
    passages, spans = mesh.shape["passage"], mesh.shape["span"]
    pairs = spans // 2
    nrows = grad_rows.shape[0]
    blocks = nx * ny * 2
    key = dest_rank[:, 0] * blocks + (dest_block % 2) * (blocks // 2) + dest_block // 2
    rows = grad_rows.transpose(1, 0, 2)
    vmem = pl.BlockSpec(memory_space=pltpu.VMEM)
    hbm = pl.BlockSpec(memory_space=pl.ANY)
    f32 = jnp.float32
    ey = ny + 16
    cx, ecy = nx // 2, ny // 2 + 16
    return pl.pallas_call(
        functools.partial(kernel, passages, spans),
        out_shape=jax.ShapeDtypeStruct((3, nx, ny, nz), f32),
        in_specs=[hbm, hbm, hbm, pl.BlockSpec(memory_space=pltpu.SMEM)],
        out_specs=vmem,
        scratch_shapes=[
            pltpu.VMEM((1, nrows), jnp.int32),
            pltpu.VMEM((3, nrows, half), f32),
            pltpu.VMEM((nx, ny, nz), jnp.int32),
            pltpu.SemaphoreType.DMA((5,)),
            pltpu.VMEM((3, nrows, nz), jnp.bfloat16),
            pltpu.VMEM((pairs, 3, blocks, half), f32),
            pltpu.VMEM((pairs, 3, blocks, half), f32),
            pltpu.VMEM((pairs - 1, 3, blocks, half), f32),
            pltpu.VMEM((pairs - 1, 3, blocks, half), f32),
            pltpu.VMEM((3, blocks, half), f32),
            pltpu.VMEM((nx + 2 * HALO_S, ey, nz), f32),
            pltpu.VMEM((3, nx + 2 * HALO_F, ey, nz), f32),
            pltpu.VMEM((3, nx + 4, ey, nz), f32),
            pltpu.VMEM((4, 3, cx + 2 * HALO_C, ecy, half), f32),
            pltpu.VMEM((nx, ny, nz), f32),
            pltpu.VMEM((6, nx + 4, ey, nz), f32),
            pltpu.VMEM((nx + 4, ey, nz), f32),
            pltpu.VMEM((6, cx + 6, ecy, half), f32),
            pltpu.VMEM((cx + 6, ecy, half), f32),
            pltpu.VMEM((7, ey, half), f32),
            pltpu.VMEM((ey, half), f32),
            pltpu.VMEM((nx + 2, ey, nz), f32),
            pltpu.SemaphoreType.DMA((pairs, 3)),
            pltpu.SemaphoreType.DMA((pairs, 3)),
            pltpu.SemaphoreType.DMA((pairs - 1, 3)),
            pltpu.SemaphoreType.DMA((pairs - 1, 3)),
            pltpu.SemaphoreType.DMA((8,)),
            pltpu.SemaphoreType.DMA((8,)),
            pltpu.SemaphoreType.DMA((3, 8)),
            pltpu.SemaphoreType.DMA((3, 8)),
            pltpu.SemaphoreType.DMA((3, 8)),
            pltpu.SemaphoreType.DMA((3, 8)),
        ],
        compiler_params=pltpu.CompilerParams(
            collective_id=0, has_side_effects=True, vmem_limit_bytes=60 * 1024 * 1024
        ),
    )(key[None, :], rows, cell_class, class_stiffness[None, :])


def solution(mesh):
    placed = (
        P(("passage", "span"), None, None),
        P(("passage", "span"), None),
        P(("passage", "span")),
        P("passage", "span", None),
        P(),
    )
    return jax.shard_map(
        functools.partial(shards, mesh),
        mesh=mesh,
        in_specs=placed,
        out_specs=P(None, "passage", "span", None),
        check_vma=False,
    )
```
